32 devices in a mesh: lon: 2 (over y), lat: 16 (over z, x, core).
Axes of the slice: x: 2, y: 2, z: 4, core: 2. Of those that a mesh axis runs over, the one named last changes fastest.
Arguments:
- state: float32 [5, 32, 192, 2880], P(None, None, 'lat', 'lon'), may hold values from -6 to 6
- decay: float32 [32, 192, 2880], P(None, 'lat', 'lon'), may hold values from 0.48 to 1, as said below
- band_rows: int32 [64], replicated, may hold values from 0 to 191, as said below
Outputs:
- advanced: float32 [5, 32, 192, 2880], P(None, None, 'lat', 'lon')
The draws below stay inside these ranges and needn't reach their ends.
Inputs may be any that keep to these rules, and one draw needn't show every extreme that they name: `band_rows`: the first m rows of the grid and the last 64 - m rows, for some m from 16 to 48. `decay`: every entry is at most 1 - 1 / 5760, so the product over a row's 2880 columns is at most exp(-1/2).
All inputs are finite; a program needn't handle non-finite values.
Results may differ from the reference program's by a relative error of at most 0.0003.
Values sent between devices are 32-bit elements; how exact they have to be, the bound alone decides.
A program may use at most 384 MiB of HBM per device.

```python
import jax
import jax.numpy as jnp
from jax import lax

MERIDIAN_CELLS = 2880
VERTICAL_LAYERS = 32
FIELDS = 5
SUBSTEPS = 2
PARALLEL_LINES = 192
NBAND = 64


def draw_decay(key, part):
    seeded_draws = jax.random.split(key, 5)
    fast_share = 0.5
    chosen = jax.random.uniform(seeded_draws[0], (VERTICAL_LAYERS, PARALLEL_LINES, 1)) < fast_share
    memory = jnp.exp(jax.random.uniform(seeded_draws[1], (VERTICAL_LAYERS, PARALLEL_LINES, 1), minval=jnp.log(30.0), maxval=jnp.log(50.0)))
    slowness = jax.random.uniform(seeded_draws[2], (VERTICAL_LAYERS, PARALLEL_LINES, 1), minval=0.5, maxval=2.0)
    expected_outcome = jnp.where(chosen, 1.0 - 1.0 / memory, 1.0 - slowness / MERIDIAN_CELLS)
    batched_sets = jax.random.uniform(seeded_draws[3], (VERTICAL_LAYERS, PARALLEL_LINES, MERIDIAN_CELLS)) < 4.0 / MERIDIAN_CELLS
    smoothing_passes = jax.random.uniform(seeded_draws[4], (VERTICAL_LAYERS, PARALLEL_LINES, MERIDIAN_CELLS), minval=0.5, maxval=0.8)
    return (expected_outcome * jnp.where(batched_sets, smoothing_passes, 1.0)).astype(jnp.float32)


def draw_band_rows(key, part):
    boundary = jax.random.randint(key, (), NBAND // 4, 3 * NBAND // 4 + 1)
    order = jnp.arange(NBAND, dtype=jnp.int32)
    return jnp.where(order < boundary, order, PARALLEL_LINES - NBAND + order).astype(jnp.int32)


def block_levels(stream_key, extent, cuts, smallest, largest):
    factor_of = 1.0
    for axis_at, blocks in cuts:
        steps = jax.random.uniform(jax.random.fold_in(jax.random.fold_in(stream_key, 6), axis_at), (blocks,), jnp.float32, smallest / len(cuts), largest / len(cuts))
        factor_of = factor_of * jnp.repeat(jnp.exp(steps), extent[axis_at] // blocks).reshape((-1,) + (1,) * (len(extent) - 1 - axis_at))
    return factor_of


def normal_values(stream_key, dims, deviation, bound, shards=(), kind=jnp.bfloat16):
    values = jax.random.normal(stream_key, dims, jnp.float32) * deviation
    if len(shards) > 0:
        values = block_levels(stream_key, dims, shards, -0.22, 0.18) * values
    return jnp.clip(values, min=-bound, max=bound).astype(kind)


def setup_inputs(seed: int = 0) -> dict:
    seeds = jax.random.split(jax.random.key(seed), 4)
    state = normal_values(seeds[0], (FIELDS, VERTICAL_LAYERS, PARALLEL_LINES, MERIDIAN_CELLS), 1.0, 6.0, ((2, 16), (3, 2)), jnp.float32)
    decay = draw_decay(jax.random.fold_in(seeds[3], 71), 0)
    band_rows = draw_band_rows(jax.random.fold_in(seeds[3], 71), 0)
    return {"state": state, "decay": decay, "band_rows": band_rows}


time_step = 0.2
coriolis = 0.5
edge_cosine = 0.5

def angles(index, count):
    return jnp.pi * index.astype(jnp.float32) / count

def faces_of(padded, axis):
    length = padded.shape[axis] - 4

    def portion(begin):
        return lax.slice_in_dim(padded, begin, begin + length + 1, axis=axis)
    return (7.0 * (portion(1) + portion(2)) - (portion(0) + portion(3))) / 12.0

def slope_of(padded, axis):
    length = padded.shape[axis] - 4

    def portion(begin):
        return lax.slice_in_dim(padded, begin, begin + length, axis=axis)
    return (8.0 * (portion(3) - portion(1)) - (portion(4) - portion(0))) / 12.0

def difference(faces, axis):
    length = faces.shape[axis] - 1
    return lax.slice_in_dim(faces, 1, length + 1, axis=axis) - lax.slice_in_dim(faces, 0, length, axis=axis)

def tendency(lon_padded, lat_padded, cosine, sine, face_cos):
    carried = jnp.stack([lon_padded[0], lon_padded[3], lon_padded[4]]) * lon_padded[1]
    zonal_part = difference(faces_of(carried, -1), -1)
    lifted = jnp.stack([lat_padded[0], lat_padded[3], lat_padded[4]]) * lat_padded[2]
    merid_part = difference(face_cos * faces_of(lifted, -2), -2)
    advected = -(zonal_part + merid_part) / cosine
    zonal_wind = lat_padded[1][..., 2:-2, :]
    merid_wind = lat_padded[2][..., 2:-2, :]
    zonal_force = -slope_of(lon_padded[0], -1) / cosine + coriolis * sine * merid_wind
    merid_force = -slope_of(lat_padded[0], -2) - coriolis * sine * zonal_wind
    return jnp.stack([advected[0], zonal_force, merid_force, advected[1], advected[2]])

def cyclic(values, rates_table):
    gain = jnp.sqrt(1.0 - rates_table * rates_table)
    driven = jnp.moveaxis(gain * values, -1, 0)
    columns = jnp.moveaxis(rates_table, -1, 0)

    def advance(carry, column):
        rate, forcing = column
        carry = rate * carry + forcing
        return (carry, carry)
    start = jnp.zeros(values.shape[:-1], jnp.float32)
    ending, unused = lax.scan(advance, start, (columns, driven))
    product = jnp.prod(rates_table, axis=-1)
    inflow = ending / (1.0 - product)
    finish, history = lax.scan(advance, inflow, (columns, driven))
    return jnp.moveaxis(history, 0, -1)

def advance_level(fields, level_decay, band_rows):
    rows = jnp.arange(PARALLEL_LINES, dtype=jnp.int32)
    centre = angles(2 * rows + 1, 2 * PARALLEL_LINES)
    cosine = jnp.sin(centre)[:, None]
    sine = -jnp.cos(centre)[:, None]
    face_cos = jnp.sin(angles(jnp.arange(PARALLEL_LINES + 1, dtype=jnp.int32), PARALLEL_LINES))[:, None]
    southern = band_rows < PARALLEL_LINES // 2
    band_cos = cosine[band_rows]
    band_decay = level_decay[band_rows]
    for substep in range(SUBSTEPS):
        lon_padded = jnp.concatenate([fields[..., -2:], fields, fields[..., :2]], axis=-1)
        lat_padded = jnp.pad(fields, ((0, 0), (2, 2), (0, 0)))
        rates = tendency(lon_padded, lat_padded, cosine, sine, face_cos)
        south_mean = lax.optimization_barrier(jnp.sum(rates[:, 0, :], axis=-1)) / MERIDIAN_CELLS
        north_mean = lax.optimization_barrier(jnp.sum(rates[:, -1, :], axis=-1)) / MERIDIAN_CELLS
        panel = jnp.where(southern[None, :], south_mean[:, None], north_mean[:, None])[:, :, None]
        picked = rates[:, band_rows, :]
        smoothed = panel + (band_cos / edge_cosine)[None] * cyclic(picked - panel, band_decay)
        rates = rates.at[:, band_rows, :].set(smoothed)
        fields = fields + time_step * rates
    return fields

def reference(state, decay, band_rows):

    def one_level(level, result):
        fields = lax.dynamic_index_in_dim(state, level, 1, keepdims=False)
        level_decay = lax.dynamic_index_in_dim(decay, level, 0, keepdims=False)
        updated = advance_level(fields, level_decay, band_rows)
        return lax.dynamic_update_index_in_dim(result, updated, level, 1)
    return lax.fori_loop(0, VERTICAL_LAYERS, one_level, jnp.zeros_like(state))
```

```python
import functools

import jax
import jax.numpy as jnp
from jax import lax
from jax.experimental import pallas as pl
from jax.experimental.pallas import tpu as pltpu
from jax.sharding import PartitionSpec as P

SUBSTEPS = 2
LANES = 128
LEVELS = 8

time_step = 0.2
coriolis = 0.5
edge_cosine = 0.5


def angles(index, count):
    return jnp.pi * index.astype(jnp.float32) / count


def lane_scan(scale, offsets, lane, steps):
    for step in range(steps):
        stride = 1 << step
        reached = lane >= stride
        masked = jnp.where(reached, scale, 0.0)
        offsets = [o + masked * pltpu.roll(o, stride, axis=1) for o in offsets]
        scale = jnp.where(reached, scale * pltpu.roll(scale, stride, axis=1), scale)
    return scale, offsets


def rates_kernel(first, band_ref, tab_ref, state_ref, tail_ref, south_ref, north_ref,
                 decay_ref, decay_tail_ref, *refs):
    if first:
        out_ref, prefix_ref, sums_ref, scale_ref, ones_ref, prefix_scale_ref, prefix_ones_ref, prod = refs
    else:
        out_ref, prefix_ref, sums_ref, prod = refs
    rows = state_ref.shape[1]
    cols = state_ref.shape[3]
    main = cols // LANES * LANES
    chunks = main // LANES + 1
    width = chunks * LANES
    lane = lax.broadcasted_iota(jnp.int32, (LEVELS, LANES), 1)
    wide_lane = lax.broadcasted_iota(jnp.int32, (LEVELS, width), 1)
    chunk_steps = max(1, (chunks - 1).bit_length())

    for part in range(4):
        for k in range(2):
            prod[part, k, :, :cols] = south_ref[part, k]
            prod[part, rows + 2 + k, :, :cols] = north_ref[part, k]

    def products(r, carry):
        merid = state_ref[2, r]
        thick = state_ref[0, r]
        prod[0, r + 2, :, :cols] = thick
        prod[1, r + 2, :, :cols] = thick * merid
        prod[2, r + 2, :, :cols] = state_ref[3, r] * merid
        prod[3, r + 2, :, :cols] = state_ref[4, r] * merid
        return carry

    lax.fori_loop(0, rows, products, 0)

    def put(ref, index, value):
        ref[index + (slice(None), slice(0, main))] = value[:, :main]
        ref[index + (slice(None), slice(main, cols))] = value[:, main:cols]

    def row(r, carry):
        def wide(f):
            return jnp.concatenate([state_ref[f, r, :, :main], tail_ref[f, r]], axis=1)

        def slope(q):
            near = pltpu.roll(q, width - 1, axis=1) - pltpu.roll(q, 1, axis=1)
            far = pltpu.roll(q, width - 2, axis=1) - pltpu.roll(q, 2, axis=1)
            return 8.0 * near - far

        lon_factor = tab_ref[r, 5]
        turn = tab_ref[r, 6]
        amount = tab_ref[r, 7]
        thick, zonal, merid = wide(0), wide(1), wide(2)
        heat, tracer = wide(3), wide(4)

        def advect(part, w):
            total = lon_factor * slope(w * zonal)
            for k in range(5):
                total = total + tab_ref[r, k] * prod[part, r + k]
            return total

        lat_slope = 8.0 * (prod[0, r + 3] - prod[0, r + 1]) - (prod[0, r + 4] - prod[0, r])
        rates = [
            advect(1, thick),
            lon_factor * slope(thick) + turn * merid,
            lat_slope * (-1.0 / 12.0) - turn * zonal,
            advect(2, heat),
            advect(3, tracer),
        ]
        rates = [jnp.where(wide_lane < cols, x, 0.0) for x in rates]

        def put_sums(side):
            for f in range(5):
                total = rates[f][:, :LANES]
                for k in range(1, chunks):
                    total = total + rates[f][:, k * LANES:(k + 1) * LANES]
                sums_ref[f, side] = total

        pl.when(r == 0)(lambda: put_sums(0))
        pl.when(r == rows - 1)(lambda: put_sums(1))
        in_band = band_ref[r] > 0
        state = [thick, zonal, merid, heat, tracer]

        @pl.when(jnp.logical_not(in_band))
        def _():
            for f in range(5):
                put(out_ref, (f, r), state[f] + time_step * rates[f])
            if first:
                zero = jnp.zeros((LEVELS, width), jnp.float32)
                put(scale_ref, (r,), zero)
                put(ones_ref, (r,), zero)

        @pl.when(in_band)
        def _():
            count = 6 if first else 5
            whole_scale = jnp.ones((LEVELS, LANES), jnp.float32)
            whole = [jnp.zeros((LEVELS, LANES), jnp.float32) for _ in range(count)]
            for k in range(chunks):
                low, high = k * LANES, (k + 1) * LANES
                last = k == chunks - 1
                decay = decay_tail_ref[r] if last else decay_ref[r, :, low:high]
                gain = jnp.sqrt(1.0 - decay * decay)
                offsets = [gain * x[:, low:high] for x in rates]
                if first:
                    offsets.append(gain)
                scale, offsets = lane_scan(decay, offsets, lane, 7)
                here = lane == k
                to_lane = (k + 1) % LANES
                whole_scale = jnp.where(here, pltpu.roll(scale, to_lane, axis=1), whole_scale)
                whole = [
                    jnp.where(here, pltpu.roll(o, to_lane, axis=1), w)
                    for o, w in zip(offsets, whole)
                ]
                end = cols if last else high
                n = end - low
                for f in range(5):
                    value = state[f][:, low:high] + amount * offsets[f]
                    out_ref[f, r, :, low:end] = value[:, :n]
                if first:
                    scale_ref[r, :, low:end] = scale[:, :n]
                    ones_ref[r, :, low:end] = (time_step - amount * offsets[5])[:, :n]
            whole_scale, whole = lane_scan(whole_scale, whole, lane, chunk_steps)
            start = lane == 0
            before = [jnp.where(start, 0.0, pltpu.roll(w, 1, axis=1)) for w in whole]
            for f in range(5):
                prefix_ref[f, r] = before[f]
            if first:
                prefix_scale_ref[r] = jnp.where(start, 1.0, pltpu.roll(whole_scale, 1, axis=1))
                prefix_ones_ref[r] = before[5]

        return carry

    lax.fori_loop(0, rows, row, 0)


def apply_kernel(state_ref, scale_ref, ones_ref, entry_ref, out_ref):
    rows = state_ref.shape[1]
    cols = state_ref.shape[3]
    main = cols // LANES * LANES
    chunks = main // LANES + 1

    def row(r, carry):
        for f in range(5):
            entry = entry_ref[f, r]
            panel = jnp.broadcast_to(entry[:, LANES - 1:], (LEVELS, LANES))
            for k in range(chunks):
                low = k * LANES
                end = min(low + LANES, cols)
                inflow = jnp.broadcast_to(entry[:, k:k + 1], (LEVELS, LANES))
                out_ref[f, r, :, low:end] = (
                    state_ref[f, r, :, low:end]
                    + scale_ref[r, :, low:end] * inflow[:, :end - low]
                    + ones_ref[r, :, low:end] * panel[:, :end - low]
                )
        return carry

    lax.fori_loop(0, rows, row, 0)


def level_block(shape):
    lead = len(shape) - 2
    return pl.BlockSpec(
        tuple(shape[:-2]) + (LEVELS, shape[-1]), lambda g: (0,) * lead + (g, 0)
    )


def shaped(shape):
    return jax.ShapeDtypeStruct(shape, jnp.float32)


def call_rates(first, band, table, state, tail, south, north, decay, decay_tail):
    fields, rows, levels, cols = state.shape
    width = cols // LANES * LANES + LANES
    outs = [
        shaped(state.shape),
        shaped((fields, rows, levels, LANES)),
        shaped((fields, 2, levels, LANES)),
    ]
    if first:
        outs += [shaped((rows, levels, cols))] * 2 + [shaped((rows, levels, LANES))] * 2
    arrays = (state, tail, south, north, decay, decay_tail)
    smem = pl.BlockSpec(memory_space=pltpu.SMEM)
    return pl.pallas_call(
        functools.partial(rates_kernel, first),
        grid=(levels // LEVELS,),
        in_specs=[smem, smem] + [level_block(x.shape) for x in arrays],
        out_specs=[level_block(x.shape) for x in outs],
        out_shape=outs,
        scratch_shapes=[pltpu.VMEM((4, rows + 4, LEVELS, width), jnp.float32)],
        compiler_params=pltpu.CompilerParams(vmem_limit_bytes=48 * 1024 * 1024),
    )(band, table, *arrays)


def call_apply(state, scale, ones, entry):
    levels = state.shape[2]
    arrays = (state, scale, ones, entry)
    return pl.pallas_call(
        apply_kernel,
        grid=(levels // LEVELS,),
        in_specs=[level_block(x.shape) for x in arrays],
        out_specs=level_block(state.shape),
        out_shape=shaped(state.shape),
        compiler_params=pltpu.CompilerParams(vmem_limit_bytes=48 * 1024 * 1024),
    )(*arrays)


def shift(x, axis, step, closed):
    count = lax.axis_size(axis)
    if closed:
        pairs = [(i, (i + step) % count) for i in range(count)]
    else:
        pairs = [(i, i + step) for i in range(count) if 0 <= i + step < count]
    return lax.ppermute(x, axis, pairs)


def lon_halos(state):
    cols = state.shape[3]
    head = jnp.moveaxis(state[..., :2], 3, 0)
    tail = jnp.moveaxis(state[..., cols - 2:], 3, 0)
    if lax.axis_size("lon") == 2:
        both = shift(jnp.concatenate([head, tail]), "lon", 1, True)
        west, east = both[2:], both[:2]
    else:
        west = shift(tail, "lon", 1, True)
        east = shift(head, "lon", -1, True)
    return jnp.moveaxis(west, 0, 3), jnp.moveaxis(east, 0, 3)


def lat_halos(state):
    rows = state.shape[1]

    def parts(strip):
        return jnp.stack(
            [strip[0], strip[0] * strip[2], strip[3] * strip[2], strip[4] * strip[2]]
        )

    south = shift(parts(state[:, rows - 2:]), "lat", 1, False)
    north = shift(parts(state[:, :2]), "lat", -1, False)
    return south, north


def over_lon(x):
    if lax.axis_size("lon") == 2:
        other = shift(x, "lon", 1, True)
        mine = lax.axis_index("lon") == 0
        return [jnp.where(mine, x, other), jnp.where(mine, other, x)]
    everything = lax.all_gather(x, "lon")
    return [everything[k] for k in range(lax.axis_size("lon"))]


def per_device(state, decay, band_rows):
    state = jnp.transpose(state, (0, 2, 1, 3))
    decay = jnp.transpose(decay, (1, 0, 2))
    fields, local_rows, levels, cols = state.shape
    lat_count, lon_count = lax.axis_size("lat"), lax.axis_size("lon")
    total_rows = local_rows * lat_count
    total_cols = cols * lon_count
    main = cols // LANES * LANES
    chunks = main // LANES + 1
    spare = main + LANES - cols - 4
    lat_index, lon_index = lax.axis_index("lat"), lax.axis_index("lon")
    rows = lat_index * local_rows + jnp.arange(local_rows, dtype=jnp.int32)
    centre = angles(2 * rows + 1, 2 * total_rows)
    cosine = jnp.sin(centre)
    sine = -jnp.cos(centre)
    face_rows = lat_index * local_rows + jnp.arange(local_rows + 1, dtype=jnp.int32)
    face_cos = jnp.sin(angles(face_rows, total_rows))
    low, high = face_cos[:-1], face_cos[1:]
    over = -1.0 / (12.0 * cosine)
    amount = time_step * cosine / edge_cosine
    table = jnp.stack(
        [
            low * over,
            (-high - 7.0 * low) * over,
            7.0 * (high - low) * over,
            (7.0 * high + low) * over,
            -high * over,
            over,
            coriolis * sine,
            amount,
        ],
        axis=1,
    )
    in_band = jnp.any(rows[:, None] == band_rows[None, :], axis=1)
    band = in_band.astype(jnp.int32)
    southern = rows < total_rows // 2
    ends = jnp.stack([lat_index == 0, lat_index == lat_count - 1])
    decay_tail = jnp.pad(
        decay[:, :, main:], ((0, 0), (0, 0), (0, main + LANES - cols)), constant_values=1.0
    )
    lanes = jnp.arange(LANES)
    gap = jnp.zeros((fields, local_rows, levels, spare), jnp.float32)
    for substep in range(SUBSTEPS):
        south, north = lat_halos(state)
        west, east = lon_halos(state)
        tail = jnp.concatenate([state[..., main:], east, gap, west], axis=3)
        outs = call_rates(
            substep == 0, band, table, state, tail, south, north, decay, decay_tail
        )
        if substep == 0:
            partial, prefix, sums, scale, ones, prefix_scale, prefix_ones = outs
        else:
            partial, prefix, sums = outs
        caps = jnp.where(ends[None, :, None], jnp.sum(sums, axis=-1), 0.0)
        caps = lax.psum(caps, ("lon", "lat")) / total_cols
        maps = jnp.concatenate(
            [
                prefix[..., chunks],
                prefix_scale[None, ..., chunks],
                prefix_ones[None, ..., chunks],
            ]
        )
        maps = over_lon(maps)
        panel = jnp.where(southern[None, :, None], caps[:, None, 0], caps[:, None, 1])
        pre_scale, pre_offset = jnp.ones_like(maps[0][:1]), jnp.zeros_like(panel)
        all_scale, all_offset = pre_scale, pre_offset
        for k in range(lon_count):
            step_scale = maps[k][5:6]
            step_offset = maps[k][:5] - panel * maps[k][6:]
            all_offset = step_scale * all_offset + step_offset
            all_scale = step_scale * all_scale
            reached = k < lon_index
            pre_scale = jnp.where(reached, all_scale, pre_scale)
            pre_offset = jnp.where(reached, all_offset, pre_offset)
        inflow = pre_scale * (all_offset / (1.0 - all_scale)) + pre_offset
        entry = amount[:, None, None] * (
            prefix
            + prefix_scale[None] * inflow[..., None]
            - panel[..., None] * prefix_ones[None]
        )
        entry = jnp.where(lanes == LANES - 1, panel[..., None], entry)
        entry = jnp.where(in_band[:, None, None], entry, 0.0)
        state = call_apply(partial, scale, ones, entry)
    return jnp.transpose(state, (0, 2, 1, 3))


def solution(mesh):
    placed = (P(None, None, "lat", "lon"), P(None, "lat", "lon"), P())
    return jax.shard_map(
        per_device,
        mesh=mesh,
        in_specs=placed,
        out_specs=P(None, None, "lat", "lon"),
        check_vma=False,
    )
```

```python
import functools

import jax
import jax.numpy as jnp
from jax import lax
from jax.experimental import pallas as pl
from jax.experimental.pallas import tpu as pltpu
from jax.sharding import PartitionSpec as P

SUBSTEPS = 2
LANES = 128
LEVELS = 8

time_step = 0.2
coriolis = 0.5
edge_cosine = 0.5


def angles(index, count):
    return jnp.pi * index.astype(jnp.float32) / count


def lane_scan(scale, offsets, lane, steps):
    for step in range(steps):
        stride = 1 << step
        reached = lane >= stride
        masked = jnp.where(reached, scale, 0.0)
        offsets = [o + masked * pltpu.roll(o, stride, axis=1) for o in offsets]
        scale = jnp.where(reached, scale * pltpu.roll(scale, stride, axis=1), scale)
    return scale, offsets


def rates_kernel(first, band_ref, tab_ref, state_ref, tail_ref, south_ref, north_ref,
                 decay_ref, decay_tail_ref, *refs):
    if first:
        out_ref, prefix_ref, sums_ref, scale_ref, ones_ref, prefix_scale_ref, prefix_ones_ref, prod = refs
    else:
        out_ref, prefix_ref, sums_ref, prod = refs
    rows = state_ref.shape[1]
    cols = state_ref.shape[3]
    main = cols // LANES * LANES
    chunks = main // LANES + 1
    width = chunks * LANES
    lane = lax.broadcasted_iota(jnp.int32, (LEVELS, LANES), 1)
    wide_lane = lax.broadcasted_iota(jnp.int32, (LEVELS, width), 1)
    chunk_steps = max(1, (chunks - 1).bit_length())

    for part in range(4):
        for k in range(2):
            prod[part, k, :, :cols] = south_ref[part, k]
            prod[part, rows + 2 + k, :, :cols] = north_ref[part, k]

    def products(r, carry):
        merid = state_ref[2, r]
        thick = state_ref[0, r]
        prod[0, r + 2, :, :cols] = thick
        prod[1, r + 2, :, :cols] = thick * merid
        prod[2, r + 2, :, :cols] = state_ref[3, r] * merid
        prod[3, r + 2, :, :cols] = state_ref[4, r] * merid
        return carry

    lax.fori_loop(0, rows, products, 0)

    def put(ref, index, value):
        ref[index + (slice(None), slice(0, main))] = value[:, :main]
        ref[index + (slice(None), slice(main, cols))] = value[:, main:cols]

    def row(r, carry):
        def wide(f):
            return jnp.concatenate([state_ref[f, r, :, :main], tail_ref[f, r]], axis=1)

        def slope(q):
            near = pltpu.roll(q, width - 1, axis=1) - pltpu.roll(q, 1, axis=1)
            far = pltpu.roll(q, width - 2, axis=1) - pltpu.roll(q, 2, axis=1)
            return 8.0 * near - far

        lon_factor = tab_ref[r, 5]
        turn = tab_ref[r, 6]
        amount = tab_ref[r, 7]
        thick, zonal, merid = wide(0), wide(1), wide(2)
        heat, tracer = wide(3), wide(4)

        def advect(part, w):
            total = lon_factor * slope(w * zonal)
            for k in range(5):
                total = total + tab_ref[r, k] * prod[part, r + k]
            return total

        lat_slope = 8.0 * (prod[0, r + 3] - prod[0, r + 1]) - (prod[0, r + 4] - prod[0, r])
        rates = [
            advect(1, thick),
            lon_factor * slope(thick) + turn * merid,
            lat_slope * (-1.0 / 12.0) - turn * zonal,
            advect(2, heat),
            advect(3, tracer),
        ]
        rates = [jnp.where(wide_lane < cols, x, 0.0) for x in rates]

        def put_sums(side):
            for f in range(5):
                total = rates[f][:, :LANES]
                for k in range(1, chunks):
                    total = total + rates[f][:, k * LANES:(k + 1) * LANES]
                sums_ref[f, side] = total

        pl.when(r == 0)(lambda: put_sums(0))
        pl.when(r == rows - 1)(lambda: put_sums(1))
        in_band = band_ref[r] > 0
        state = [thick, zonal, merid, heat, tracer]

        @pl.when(jnp.logical_not(in_band))
        def _():
            for f in range(5):
                put(out_ref, (f, r), state[f] + time_step * rates[f])
            if first:
                zero = jnp.zeros((LEVELS, width), jnp.float32)
                put(scale_ref, (r,), zero)
                put(ones_ref, (r,), zero)

        @pl.when(in_band)
        def _():
            count = 6 if first else 5
            whole_scale = jnp.ones((LEVELS, LANES), jnp.float32)
            whole = [jnp.zeros((LEVELS, LANES), jnp.float32) for _ in range(count)]
            for k in range(chunks):
                low, high = k * LANES, (k + 1) * LANES
                last = k == chunks - 1
                decay = decay_tail_ref[r] if last else decay_ref[r, :, low:high]
                gain = jnp.sqrt(1.0 - decay * decay)
                offsets = [gain * x[:, low:high] for x in rates]
                if first:
                    offsets.append(gain)
                scale, offsets = lane_scan(decay, offsets, lane, 7)
                here = lane == k
                to_lane = (k + 1) % LANES
                whole_scale = jnp.where(here, pltpu.roll(scale, to_lane, axis=1), whole_scale)
                whole = [
                    jnp.where(here, pltpu.roll(o, to_lane, axis=1), w)
                    for o, w in zip(offsets, whole)
                ]
                end = cols if last else high
                n = end - low
                for f in range(5):
                    value = state[f][:, low:high] + amount * offsets[f]
                    out_ref[f, r, :, low:end] = value[:, :n]
                if first:
                    scale_ref[r, :, low:end] = scale[:, :n]
                    ones_ref[r, :, low:end] = (time_step - amount * offsets[5])[:, :n]
            whole_scale, whole = lane_scan(whole_scale, whole, lane, chunk_steps)
            start = lane == 0
            before = [jnp.where(start, 0.0, pltpu.roll(w, 1, axis=1)) for w in whole]
            for f in range(5):
                prefix_ref[f, r] = before[f]
            if first:
                prefix_scale_ref[r] = jnp.where(start, 1.0, pltpu.roll(whole_scale, 1, axis=1))
                prefix_ones_ref[r] = before[5]

        return carry

    lax.fori_loop(0, rows, row, 0)


def apply_kernel(state_ref, scale_ref, ones_ref, entry_ref, out_ref):
    rows = state_ref.shape[1]
    cols = state_ref.shape[3]
    main = cols // LANES * LANES
    chunks = main // LANES + 1

    def row(r, carry):
        for f in range(5):
            entry = entry_ref[f, r]
            panel = jnp.broadcast_to(entry[:, LANES - 1:], (LEVELS, LANES))
            for k in range(chunks):
                low = k * LANES
                end = min(low + LANES, cols)
                inflow = jnp.broadcast_to(entry[:, k:k + 1], (LEVELS, LANES))
                out_ref[f, r, :, low:end] = (
                    state_ref[f, r, :, low:end]
                    + scale_ref[r, :, low:end] * inflow[:, :end - low]
                    + ones_ref[r, :, low:end] * panel[:, :end - low]
                )
        return carry

    lax.fori_loop(0, rows, row, 0)


def caps_kernel(caps_ref, out_ref, send_sem, recv_sem):
    mine, count = lax.axis_index("lat"), lax.axis_size("lat")
    barrier = pltpu.get_barrier_semaphore()
    poles = (0, count - 1)

    def greet(pole):
        pl.semaphore_signal(
            barrier, inc=1, device_id={"lat": pole}, device_id_type=pl.DeviceIdType.MESH
        )

    def copy(side, other):
        return pltpu.make_async_remote_copy(
            src_ref=caps_ref.at[side],
            dst_ref=out_ref.at[side],
            send_sem=send_sem.at[other],
            recv_sem=recv_sem.at[side],
            device_id={"lat": other},
            device_id_type=pl.DeviceIdType.MESH,
        )

    for side, pole in enumerate(poles):
        pl.when(mine != pole)(functools.partial(greet, pole))
    for side, pole in enumerate(poles):

        @pl.when(mine == pole)
        def _():
            pl.semaphore_wait(barrier, count - 1)
            out_ref[side] = caps_ref[side]

            def start(step, carry):
                copy(side, lax.rem(pole + step, count)).start()
                return carry

            lax.fori_loop(1, count, start, 0)

    for side, pole in enumerate(poles):

        @pl.when(mine != pole)
        def _():
            copy(side, pole).wait_recv()

        @pl.when(mine == pole)
        def _():
            def finish(step, carry):
                copy(side, lax.rem(pole + step, count)).wait_send()
                return carry

            lax.fori_loop(1, count, finish, 0)


def share_caps(caps):
    return pl.pallas_call(
        caps_kernel,
        out_shape=shaped(caps.shape),
        in_specs=[pl.BlockSpec(memory_space=pltpu.VMEM)],
        out_specs=pl.BlockSpec(memory_space=pltpu.VMEM),
        scratch_shapes=[
            pltpu.SemaphoreType.DMA((lax.axis_size("lat"),)),
            pltpu.SemaphoreType.DMA((2,)),
        ],
        compiler_params=pltpu.CompilerParams(collective_id=0, has_side_effects=True),
    )(caps)


def level_block(shape):
    lead = len(shape) - 2
    return pl.BlockSpec(
        tuple(shape[:-2]) + (LEVELS, shape[-1]), lambda g: (0,) * lead + (g, 0)
    )


def shaped(shape):
    return jax.ShapeDtypeStruct(shape, jnp.float32)


def call_rates(first, band, table, state, tail, south, north, decay, decay_tail):
    fields, rows, levels, cols = state.shape
    width = cols // LANES * LANES + LANES
    outs = [
        shaped(state.shape),
        shaped((fields, rows, levels, LANES)),
        shaped((fields, 2, levels, LANES)),
    ]
    if first:
        outs += [shaped((rows, levels, cols))] * 2 + [shaped((rows, levels, LANES))] * 2
    arrays = (state, tail, south, north, decay, decay_tail)
    smem = pl.BlockSpec(memory_space=pltpu.SMEM)
    return pl.pallas_call(
        functools.partial(rates_kernel, first),
        grid=(levels // LEVELS,),
        in_specs=[smem, smem] + [level_block(x.shape) for x in arrays],
        out_specs=[level_block(x.shape) for x in outs],
        out_shape=outs,
        scratch_shapes=[pltpu.VMEM((4, rows + 4, LEVELS, width), jnp.float32)],
        compiler_params=pltpu.CompilerParams(vmem_limit_bytes=48 * 1024 * 1024),
    )(band, table, *arrays)


def call_apply(state, scale, ones, entry):
    levels = state.shape[2]
    arrays = (state, scale, ones, entry)
    return pl.pallas_call(
        apply_kernel,
        grid=(levels // LEVELS,),
        in_specs=[level_block(x.shape) for x in arrays],
        out_specs=level_block(state.shape),
        out_shape=shaped(state.shape),
        compiler_params=pltpu.CompilerParams(vmem_limit_bytes=48 * 1024 * 1024),
    )(*arrays)


def shift(x, axis, step, closed):
    count = lax.axis_size(axis)
    if closed:
        pairs = [(i, (i + step) % count) for i in range(count)]
    else:
        pairs = [(i, i + step) for i in range(count) if 0 <= i + step < count]
    return lax.ppermute(x, axis, pairs)


def lon_halos(state):
    cols = state.shape[3]
    head = jnp.moveaxis(state[..., :2], 3, 0)
    tail = jnp.moveaxis(state[..., cols - 2:], 3, 0)
    if lax.axis_size("lon") == 2:
        both = shift(jnp.concatenate([head, tail]), "lon", 1, True)
        west, east = both[2:], both[:2]
    else:
        west = shift(tail, "lon", 1, True)
        east = shift(head, "lon", -1, True)
    return jnp.moveaxis(west, 0, 3), jnp.moveaxis(east, 0, 3)


def lat_halos(state):
    rows = state.shape[1]

    def parts(strip):
        return jnp.stack(
            [strip[0], strip[0] * strip[2], strip[3] * strip[2], strip[4] * strip[2]]
        )

    south = shift(parts(state[:, rows - 2:]), "lat", 1, False)
    north = shift(parts(state[:, :2]), "lat", -1, False)
    return south, north


def over_lon(x):
    if lax.axis_size("lon") == 2:
        other = shift(x, "lon", 1, True)
        mine = lax.axis_index("lon") == 0
        return [jnp.where(mine, x, other), jnp.where(mine, other, x)]
    everything = lax.all_gather(x, "lon")
    return [everything[k] for k in range(lax.axis_size("lon"))]


def per_device(state, decay, band_rows):
    state = jnp.transpose(state, (0, 2, 1, 3))
    decay = jnp.transpose(decay, (1, 0, 2))
    fields, local_rows, levels, cols = state.shape
    lat_count, lon_count = lax.axis_size("lat"), lax.axis_size("lon")
    total_rows = local_rows * lat_count
    total_cols = cols * lon_count
    main = cols // LANES * LANES
    chunks = main // LANES + 1
    spare = main + LANES - cols - 4
    lat_index, lon_index = lax.axis_index("lat"), lax.axis_index("lon")
    rows = lat_index * local_rows + jnp.arange(local_rows, dtype=jnp.int32)
    centre = angles(2 * rows + 1, 2 * total_rows)
    cosine = jnp.sin(centre)
    sine = -jnp.cos(centre)
    face_rows = lat_index * local_rows + jnp.arange(local_rows + 1, dtype=jnp.int32)
    face_cos = jnp.sin(angles(face_rows, total_rows))
    low, high = face_cos[:-1], face_cos[1:]
    over = -1.0 / (12.0 * cosine)
    amount = time_step * cosine / edge_cosine
    table = jnp.stack(
        [
            low * over,
            (-high - 7.0 * low) * over,
            7.0 * (high - low) * over,
            (7.0 * high + low) * over,
            -high * over,
            over,
            coriolis * sine,
            amount,
        ],
        axis=1,
    )
    in_band = jnp.any(rows[:, None] == band_rows[None, :], axis=1)
    band = in_band.astype(jnp.int32)
    southern = rows < total_rows // 2
    decay_tail = jnp.pad(
        decay[:, :, main:], ((0, 0), (0, 0), (0, main + LANES - cols)), constant_values=1.0
    )
    lanes = jnp.arange(LANES)
    gap = jnp.zeros((fields, local_rows, levels, spare), jnp.float32)
    for substep in range(SUBSTEPS):
        south, north = lat_halos(state)
        west, east = lon_halos(state)
        tail = jnp.concatenate([state[..., main:], east, gap, west], axis=3)
        outs = call_rates(
            substep == 0, band, table, state, tail, south, north, decay, decay_tail
        )
        if substep == 0:
            partial, prefix, sums, scale, ones, prefix_scale, prefix_ones = outs
        else:
            partial, prefix, sums = outs
        caps = share_caps(jnp.moveaxis(jnp.sum(sums, axis=-1), 1, 0))
        maps = jnp.concatenate(
            [
                prefix[..., chunks],
                prefix_scale[None, ..., chunks],
                prefix_ones[None, ..., chunks],
                jnp.where(southern[None, :, None], caps[0][:, None], caps[1][:, None]),
            ]
        )
        maps = over_lon(maps)
        panel = sum(x[7:] for x in maps) / total_cols
        pre_scale, pre_offset = jnp.ones_like(maps[0][:1]), jnp.zeros_like(panel)
        all_scale, all_offset = pre_scale, pre_offset
        for k in range(lon_count):
            step_scale = maps[k][5:6]
            step_offset = maps[k][:5] - panel * maps[k][6:7]
            all_offset = step_scale * all_offset + step_offset
            all_scale = step_scale * all_scale
            reached = k < lon_index
            pre_scale = jnp.where(reached, all_scale, pre_scale)
            pre_offset = jnp.where(reached, all_offset, pre_offset)
        inflow = pre_scale * (all_offset / (1.0 - all_scale)) + pre_offset
        entry = amount[:, None, None] * (
            prefix
            + prefix_scale[None] * inflow[..., None]
            - panel[..., None] * prefix_ones[None]
        )
        entry = jnp.where(lanes == LANES - 1, panel[..., None], entry)
        entry = jnp.where(in_band[:, None, None], entry, 0.0)
        state = call_apply(partial, scale, ones, entry)
    return jnp.transpose(state, (0, 2, 1, 3))


def solution(mesh):
    placed = (P(None, None, "lat", "lon"), P(None, "lat", "lon"), P())
    return jax.shard_map(
        per_device,
        mesh=mesh,
        in_specs=placed,
        out_specs=P(None, None, "lat", "lon"),
        check_vma=False,
    )
```

```python
import functools

import jax
import jax.numpy as jnp
from jax import lax
from jax.experimental import pallas as pl
from jax.experimental.pallas import tpu as pltpu
from jax.sharding import PartitionSpec as P

SUBSTEPS = 2
LANES = 128
LEVELS = 8
EDGE = 2

time_step = 0.2
coriolis = 0.5
edge_cosine = 0.5


def angles(index, count):
    return jnp.pi * index.astype(jnp.float32) / count


def lane_scan(scale, offsets, lane, steps):
    for step in range(steps):
        stride = 1 << step
        reached = lane >= stride
        masked = jnp.where(reached, scale, 0.0)
        offsets = [o + masked * pltpu.roll(o, stride, axis=1) for o in offsets]
        scale = jnp.where(reached, scale * pltpu.roll(scale, stride, axis=1), scale)
    return scale, offsets


def rates_kernel(first, inner, band_ref, tab_ref, state_ref, tail_ref,
                 decay_ref, decay_tail_ref, *refs):
    refs = list(refs)
    if not inner:
        south_ref, north_ref = refs.pop(0), refs.pop(0)
    out_ref, prefix_ref = refs.pop(0), refs.pop(0)
    if not inner:
        sums_ref = refs.pop(0)
    if first:
        scale_ref, ones_ref, prefix_scale_ref, prefix_ones_ref = refs[:4]
    prod = refs[-1]
    rows = state_ref.shape[1]
    cols = state_ref.shape[3]
    main = cols // LANES * LANES
    chunks = main // LANES + 1
    width = chunks * LANES
    lane = lax.broadcasted_iota(jnp.int32, (LEVELS, LANES), 1)
    wide_lane = lax.broadcasted_iota(jnp.int32, (LEVELS, width), 1)
    chunk_steps = max(1, (chunks - 1).bit_length())

    for part in range(0 if inner else 4):
        for k in range(EDGE):
            prod[part, k, :, :cols] = south_ref[part, k]
            prod[part, rows + 2 + k, :, :cols] = north_ref[part, k]

    def products(r, carry):
        merid = state_ref[2, r]
        thick = state_ref[0, r]
        prod[0, r + 2, :, :cols] = thick
        prod[1, r + 2, :, :cols] = thick * merid
        prod[2, r + 2, :, :cols] = state_ref[3, r] * merid
        prod[3, r + 2, :, :cols] = state_ref[4, r] * merid
        return carry

    if inner:
        lax.fori_loop(0, rows, products, 0)
    else:
        lax.fori_loop(0, 2 * EDGE, products, 0)
        lax.fori_loop(rows - 2 * EDGE, rows, products, 0)

    def put(ref, index, value):
        ref[index + (slice(None), slice(0, main))] = value[:, :main]
        ref[index + (slice(None), slice(main, cols))] = value[:, main:cols]

    def row(i, carry):
        r = i + EDGE if inner else jnp.where(i < EDGE, i, i + (rows - 2 * EDGE))

        def wide(f):
            return jnp.concatenate([state_ref[f, r, :, :main], tail_ref[f, r]], axis=1)

        def slope(q):
            near = pltpu.roll(q, width - 1, axis=1) - pltpu.roll(q, 1, axis=1)
            far = pltpu.roll(q, width - 2, axis=1) - pltpu.roll(q, 2, axis=1)
            return 8.0 * near - far

        lon_factor = tab_ref[r, 5]
        turn = tab_ref[r, 6]
        amount = tab_ref[r, 7]
        thick, zonal, merid = wide(0), wide(1), wide(2)
        heat, tracer = wide(3), wide(4)

        def advect(part, w):
            total = lon_factor * slope(w * zonal)
            for k in range(5):
                total = total + tab_ref[r, k] * prod[part, r + k]
            return total

        lat_slope = 8.0 * (prod[0, r + 3] - prod[0, r + 1]) - (prod[0, r + 4] - prod[0, r])
        rates = [
            advect(1, thick),
            lon_factor * slope(thick) + turn * merid,
            lat_slope * (-1.0 / 12.0) - turn * zonal,
            advect(2, heat),
            advect(3, tracer),
        ]
        rates = [jnp.where(wide_lane < cols, x, 0.0) for x in rates]

        def put_sums(side):
            for f in range(5):
                total = rates[f][:, :LANES]
                for k in range(1, chunks):
                    total = total + rates[f][:, k * LANES:(k + 1) * LANES]
                sums_ref[f, side] = total

        if not inner:
            pl.when(r == 0)(lambda: put_sums(0))
            pl.when(r == rows - 1)(lambda: put_sums(1))
        in_band = band_ref[r] > 0
        state = [thick, zonal, merid, heat, tracer]

        @pl.when(jnp.logical_not(in_band))
        def _():
            for f in range(5):
                put(out_ref, (f, i), state[f] + time_step * rates[f])
            if first:
                zero = jnp.zeros((LEVELS, width), jnp.float32)
                put(scale_ref, (i,), zero)
                put(ones_ref, (i,), zero)

        @pl.when(in_band)
        def _():
            count = 6 if first else 5
            whole_scale = jnp.ones((LEVELS, LANES), jnp.float32)
            whole = [jnp.zeros((LEVELS, LANES), jnp.float32) for _ in range(count)]
            for k in range(chunks):
                low, high = k * LANES, (k + 1) * LANES
                last = k == chunks - 1
                decay = decay_tail_ref[r] if last else decay_ref[r, :, low:high]
                gain = jnp.sqrt(1.0 - decay * decay)
                offsets = [gain * x[:, low:high] for x in rates]
                if first:
                    offsets.append(gain)
                scale, offsets = lane_scan(decay, offsets, lane, 7)
                here = lane == k
                to_lane = (k + 1) % LANES
                whole_scale = jnp.where(here, pltpu.roll(scale, to_lane, axis=1), whole_scale)
                whole = [
                    jnp.where(here, pltpu.roll(o, to_lane, axis=1), w)
                    for o, w in zip(offsets, whole)
                ]
                end = cols if last else high
                n = end - low
                for f in range(5):
                    value = state[f][:, low:high] + amount * offsets[f]
                    out_ref[f, i, :, low:end] = value[:, :n]
                if first:
                    scale_ref[i, :, low:end] = scale[:, :n]
                    ones_ref[i, :, low:end] = (time_step - amount * offsets[5])[:, :n]
            whole_scale, whole = lane_scan(whole_scale, whole, lane, chunk_steps)
            start = lane == 0
            before = [jnp.where(start, 0.0, pltpu.roll(w, 1, axis=1)) for w in whole]
            for f in range(5):
                prefix_ref[f, i] = before[f]
            if first:
                prefix_scale_ref[i] = jnp.where(start, 1.0, pltpu.roll(whole_scale, 1, axis=1))
                prefix_ones_ref[i] = before[5]

        return carry

    lax.fori_loop(0, rows - 2 * EDGE if inner else 2 * EDGE, row, 0)


def apply_kernel(state_ref, scale_ref, ones_ref, edge_state_ref, edge_scale_ref, edge_ones_ref,
                 entry_ref, out_ref):
    rows = out_ref.shape[1]
    inner = (state_ref, scale_ref, ones_ref)
    edges = (edge_state_ref, edge_scale_ref, edge_ones_ref)
    lax.fori_loop(
        0, rows - 2 * EDGE, functools.partial(apply_row, *inner, entry_ref, out_ref, EDGE), 0
    )
    lax.fori_loop(0, EDGE, functools.partial(apply_row, *edges, entry_ref, out_ref, 0), 0)
    lax.fori_loop(
        EDGE,
        2 * EDGE,
        functools.partial(apply_row, *edges, entry_ref, out_ref, rows - 2 * EDGE),
        0,
    )


def apply_row(state_ref, scale_ref, ones_ref, entry_ref, out_ref, shift_by, i, carry):
    cols = state_ref.shape[3]
    main = cols // LANES * LANES
    chunks = main // LANES + 1

    r = i + shift_by
    for f in range(5):
        entry = entry_ref[f, r]
        panel = jnp.broadcast_to(entry[:, LANES - 1:], (LEVELS, LANES))
        for k in range(chunks):
            low = k * LANES
            end = min(low + LANES, cols)
            inflow = jnp.broadcast_to(entry[:, k:k + 1], (LEVELS, LANES))
            out_ref[f, r, :, low:end] = (
                state_ref[f, i, :, low:end]
                + scale_ref[i, :, low:end] * inflow[:, :end - low]
                + ones_ref[i, :, low:end] * panel[:, :end - low]
            )
    return carry


def caps_kernel(caps_ref, out_ref, send_sem, recv_sem):
    mine, count = lax.axis_index("lat"), lax.axis_size("lat")
    barrier = pltpu.get_barrier_semaphore()
    poles = (0, count - 1)

    def greet(pole):
        pl.semaphore_signal(
            barrier, inc=1, device_id={"lat": pole}, device_id_type=pl.DeviceIdType.MESH
        )

    def copy(side, other):
        return pltpu.make_async_remote_copy(
            src_ref=caps_ref.at[side],
            dst_ref=out_ref.at[side],
            send_sem=send_sem.at[other],
            recv_sem=recv_sem.at[side],
            device_id={"lat": other},
            device_id_type=pl.DeviceIdType.MESH,
        )

    for side, pole in enumerate(poles):
        pl.when(mine != pole)(functools.partial(greet, pole))
    for side, pole in enumerate(poles):

        @pl.when(mine == pole)
        def _():
            pl.semaphore_wait(barrier, count - 1)
            out_ref[side] = caps_ref[side]

            def start(step, carry):
                copy(side, lax.rem(pole + step, count)).start()
                return carry

            lax.fori_loop(1, count, start, 0)

    for side, pole in enumerate(poles):

        @pl.when(mine != pole)
        def _():
            copy(side, pole).wait_recv()

        @pl.when(mine == pole)
        def _():
            def finish(step, carry):
                copy(side, lax.rem(pole + step, count)).wait_send()
                return carry

            lax.fori_loop(1, count, finish, 0)


def share_caps(caps):
    return pl.pallas_call(
        caps_kernel,
        out_shape=shaped(caps.shape),
        in_specs=[pl.BlockSpec(memory_space=pltpu.VMEM)],
        out_specs=pl.BlockSpec(memory_space=pltpu.VMEM),
        scratch_shapes=[
            pltpu.SemaphoreType.DMA((lax.axis_size("lat"),)),
            pltpu.SemaphoreType.DMA((2,)),
        ],
        compiler_params=pltpu.CompilerParams(collective_id=0, has_side_effects=True),
    )(caps)


def level_block(shape):
    lead = len(shape) - 2
    return pl.BlockSpec(
        tuple(shape[:-2]) + (LEVELS, shape[-1]), lambda g: (0,) * lead + (g, 0)
    )


def shaped(shape):
    return jax.ShapeDtypeStruct(shape, jnp.float32)


def call_rates(first, band, table, state, tail, decay, decay_tail, halos=None):
    fields, rows, levels, cols = state.shape
    width = cols // LANES * LANES + LANES
    inner = halos is None
    count = rows - 2 * EDGE if inner else 2 * EDGE
    outs = [shaped((fields, count, levels, cols)), shaped((fields, count, levels, LANES))]
    if not inner:
        outs += [shaped((fields, 2, levels, LANES))]
    if first:
        outs += [shaped((count, levels, cols))] * 2 + [shaped((count, levels, LANES))] * 2
    arrays = (state, tail, decay, decay_tail) + (() if inner else halos)
    smem = pl.BlockSpec(memory_space=pltpu.SMEM)
    cells = fields * count * levels * cols
    return pl.pallas_call(
        functools.partial(rates_kernel, first, inner),
        grid=(levels // LEVELS,),
        in_specs=[smem, smem] + [level_block(x.shape) for x in arrays],
        out_specs=[level_block(x.shape) for x in outs],
        out_shape=outs,
        scratch_shapes=[pltpu.VMEM((4, rows + 4, LEVELS, width), jnp.float32)],
        compiler_params=pltpu.CompilerParams(vmem_limit_bytes=48 * 1024 * 1024),
        cost_estimate=pl.CostEstimate(
            flops=400 * cells, bytes_accessed=40 * cells, transcendentals=0
        ),
    )(band, table, *arrays)


def call_apply(inner, edges, entry):
    fields, rows, levels, _ = entry.shape
    cols = inner[0].shape[3]
    arrays = tuple(inner) + tuple(edges) + (entry,)
    out = shaped((fields, rows, levels, cols))
    return pl.pallas_call(
        apply_kernel,
        grid=(levels // LEVELS,),
        in_specs=[level_block(x.shape) for x in arrays],
        out_specs=level_block(out.shape),
        out_shape=out,
        compiler_params=pltpu.CompilerParams(vmem_limit_bytes=48 * 1024 * 1024),
    )(*arrays)


def join_rows(inner, edges, axis):
    first = lax.slice_in_dim(edges, 0, EDGE, axis=axis)
    last = lax.slice_in_dim(edges, EDGE, 2 * EDGE, axis=axis)
    return jnp.concatenate([first, inner, last], axis=axis)


def shift(x, axis, step, closed):
    count = lax.axis_size(axis)
    if closed:
        pairs = [(i, (i + step) % count) for i in range(count)]
    else:
        pairs = [(i, i + step) for i in range(count) if 0 <= i + step < count]
    return lax.ppermute(x, axis, pairs)


def lon_halos(state):
    cols = state.shape[3]
    head = jnp.moveaxis(state[..., :2], 3, 0)
    tail = jnp.moveaxis(state[..., cols - 2:], 3, 0)
    if lax.axis_size("lon") == 2:
        both = shift(jnp.concatenate([head, tail]), "lon", 1, True)
        west, east = both[2:], both[:2]
    else:
        west = shift(tail, "lon", 1, True)
        east = shift(head, "lon", -1, True)
    return jnp.moveaxis(west, 0, 3), jnp.moveaxis(east, 0, 3)


def lat_halos(state):
    rows = state.shape[1]

    def parts(strip):
        return jnp.stack(
            [strip[0], strip[0] * strip[2], strip[3] * strip[2], strip[4] * strip[2]]
        )

    south = shift(parts(state[:, rows - 2:]), "lat", 1, False)
    north = shift(parts(state[:, :2]), "lat", -1, False)
    return south, north


def over_lon(x):
    if lax.axis_size("lon") == 2:
        other = shift(x, "lon", 1, True)
        mine = lax.axis_index("lon") == 0
        return [jnp.where(mine, x, other), jnp.where(mine, other, x)]
    everything = lax.all_gather(x, "lon")
    return [everything[k] for k in range(lax.axis_size("lon"))]


def per_device(state, decay, band_rows):
    state = jnp.transpose(state, (0, 2, 1, 3))
    decay = jnp.transpose(decay, (1, 0, 2))
    fields, local_rows, levels, cols = state.shape
    lat_count, lon_count = lax.axis_size("lat"), lax.axis_size("lon")
    total_rows = local_rows * lat_count
    total_cols = cols * lon_count
    main = cols // LANES * LANES
    chunks = main // LANES + 1
    spare = main + LANES - cols - 4
    lat_index, lon_index = lax.axis_index("lat"), lax.axis_index("lon")
    rows = lat_index * local_rows + jnp.arange(local_rows, dtype=jnp.int32)
    centre = angles(2 * rows + 1, 2 * total_rows)
    cosine = jnp.sin(centre)
    sine = -jnp.cos(centre)
    face_rows = lat_index * local_rows + jnp.arange(local_rows + 1, dtype=jnp.int32)
    face_cos = jnp.sin(angles(face_rows, total_rows))
    low, high = face_cos[:-1], face_cos[1:]
    over = -1.0 / (12.0 * cosine)
    amount = time_step * cosine / edge_cosine
    table = jnp.stack(
        [
            low * over,
            (-high - 7.0 * low) * over,
            7.0 * (high - low) * over,
            (7.0 * high + low) * over,
            -high * over,
            over,
            coriolis * sine,
            amount,
        ],
        axis=1,
    )
    in_band = jnp.any(rows[:, None] == band_rows[None, :], axis=1)
    band = in_band.astype(jnp.int32)
    southern = rows < total_rows // 2
    decay_tail = jnp.pad(
        decay[:, :, main:], ((0, 0), (0, 0), (0, main + LANES - cols)), constant_values=1.0
    )
    lanes = jnp.arange(LANES)
    gap = jnp.zeros((fields, local_rows, levels, spare), jnp.float32)
    for substep in range(SUBSTEPS):
        south, north = lat_halos(state)
        west, east = lon_halos(state)
        tail = jnp.concatenate([state[..., main:], east, gap, west], axis=3)
        common = (substep == 0, band, table, state, tail, decay, decay_tail)
        inner = list(call_rates(*common))
        edges = list(call_rates(*common, halos=(south, north)))
        sums = edges.pop(2)
        prefix = join_rows(inner[1], edges[1], 1)
        if substep == 0:
            inner_maps, edge_maps = inner[2:4], edges[2:4]
            prefix_scale = join_rows(inner[4], edges[4], 0)
            prefix_ones = join_rows(inner[5], edges[5], 0)
        caps = share_caps(jnp.moveaxis(jnp.sum(sums, axis=-1), 1, 0))
        maps = jnp.concatenate(
            [
                prefix[..., chunks],
                prefix_scale[None, ..., chunks],
                prefix_ones[None, ..., chunks],
                jnp.where(southern[None, :, None], caps[0][:, None], caps[1][:, None]),
            ]
        )
        maps = over_lon(maps)
        panel = sum(x[7:] for x in maps) / total_cols
        pre_scale, pre_offset = jnp.ones_like(maps[0][:1]), jnp.zeros_like(panel)
        all_scale, all_offset = pre_scale, pre_offset
        for k in range(lon_count):
            step_scale = maps[k][5:6]
            step_offset = maps[k][:5] - panel * maps[k][6:7]
            all_offset = step_scale * all_offset + step_offset
            all_scale = step_scale * all_scale
            reached = k < lon_index
            pre_scale = jnp.where(reached, all_scale, pre_scale)
            pre_offset = jnp.where(reached, all_offset, pre_offset)
        inflow = pre_scale * (all_offset / (1.0 - all_scale)) + pre_offset
        entry = amount[:, None, None] * (
            prefix
            + prefix_scale[None] * inflow[..., None]
            - panel[..., None] * prefix_ones[None]
        )
        entry = jnp.where(lanes == LANES - 1, panel[..., None], entry)
        entry = jnp.where(in_band[:, None, None], entry, 0.0)
        state = call_apply([inner[0]] + inner_maps, [edges[0]] + edge_maps, entry)
    return jnp.transpose(state, (0, 2, 1, 3))


def solution(mesh):
    placed = (P(None, None, "lat", "lon"), P(None, "lat", "lon"), P())
    return jax.shard_map(
        per_device,
        mesh=mesh,
        in_specs=placed,
        out_specs=P(None, None, "lat", "lon"),
        check_vma=False,
    )
```

```python
import functools

import jax
import jax.numpy as jnp
from jax import lax
from jax.experimental import pallas as pl
from jax.experimental.pallas import tpu as pltpu
from jax.sharding import PartitionSpec as P

SUBSTEPS = 2
LANES = 128
LEVELS = 8
EDGE = 2

time_step = 0.2
coriolis = 0.5
edge_cosine = 0.5


def angles(index, count):
    return jnp.pi * index.astype(jnp.float32) / count


def lane_scan(scale, offsets, lane, steps):
    for step in range(steps):
        stride = 1 << step
        reached = lane >= stride
        masked = jnp.where(reached, scale, 0.0)
        offsets = [o + masked * pltpu.roll(o, stride, axis=1) for o in offsets]
        scale = jnp.where(reached, scale * pltpu.roll(scale, stride, axis=1), scale)
    return scale, offsets


def rates_kernel(first, inner, band_ref, tab_ref, state_ref, tail_ref,
                 decay_ref, decay_tail_ref, *refs):
    refs = list(refs)
    if not inner:
        south_ref, north_ref = refs.pop(0), refs.pop(0)
    out_ref, prefix_ref = refs.pop(0), refs.pop(0)
    if not inner:
        sums_ref = refs.pop(0)
    if first:
        scale_ref, ones_ref, prefix_scale_ref, prefix_ones_ref = refs[:4]
    prod = refs[-1]
    rows = state_ref.shape[1]
    cols = state_ref.shape[3]
    main = cols // LANES * LANES
    chunks = main // LANES + 1
    width = chunks * LANES
    lane = lax.broadcasted_iota(jnp.int32, (LEVELS, LANES), 1)
    wide_lane = lax.broadcasted_iota(jnp.int32, (LEVELS, width), 1)
    chunk_steps = max(1, (chunks - 1).bit_length())

    for part in range(0 if inner else 4):
        for k in range(EDGE):
            prod[part, k, :, :cols] = south_ref[part, k]
            prod[part, rows + 2 + k, :, :cols] = north_ref[part, k]

    def products(r, carry):
        merid = state_ref[2, r]
        thick = state_ref[0, r]
        prod[0, r + 2, :, :cols] = thick
        prod[1, r + 2, :, :cols] = thick * merid
        prod[2, r + 2, :, :cols] = state_ref[3, r] * merid
        prod[3, r + 2, :, :cols] = state_ref[4, r] * merid
        return carry

    if inner:
        lax.fori_loop(0, rows, products, 0)
    else:
        lax.fori_loop(0, 2 * EDGE, products, 0)
        lax.fori_loop(rows - 2 * EDGE, rows, products, 0)

    def put(ref, index, value):
        ref[index + (slice(None), slice(0, main))] = value[:, :main]
        ref[index + (slice(None), slice(main, cols))] = value[:, main:cols]

    def row(i, carry):
        r = i + EDGE if inner else jnp.where(i < EDGE, i, i + (rows - 2 * EDGE))

        def wide(f):
            return jnp.concatenate([state_ref[f, r, :, :main], tail_ref[f, r]], axis=1)

        def slope(q):
            step = q - pltpu.roll(q, 2, axis=1)
            next_steps = pltpu.roll(step, width - 1, axis=1), pltpu.roll(step, width - 2, axis=1)
            return 8.0 * next_steps[0] - next_steps[1] - step

        lon_factor = tab_ref[r, 5]
        turn = tab_ref[r, 6]
        amount = tab_ref[r, 7]
        thick, zonal, merid = wide(0), wide(1), wide(2)
        heat, tracer = wide(3), wide(4)

        def advect(part, w):
            total = lon_factor * slope(w * zonal)
            for k in range(5):
                total = total + tab_ref[r, k] * prod[part, r + k]
            return total

        lat_slope = 8.0 * (prod[0, r + 3] - prod[0, r + 1]) - (prod[0, r + 4] - prod[0, r])
        rates = [
            advect(1, thick),
            lon_factor * slope(thick) + turn * merid,
            lat_slope * (-1.0 / 12.0) - turn * zonal,
            advect(2, heat),
            advect(3, tracer),
        ]
        rates = [jnp.where(wide_lane < cols, x, 0.0) for x in rates]

        def put_sums(side):
            for f in range(5):
                total = rates[f][:, :LANES]
                for k in range(1, chunks):
                    total = total + rates[f][:, k * LANES:(k + 1) * LANES]
                sums_ref[f, side] = total

        if not inner:
            pl.when(r == 0)(lambda: put_sums(0))
            pl.when(r == rows - 1)(lambda: put_sums(1))
        in_band = band_ref[r] > 0
        state = [thick, zonal, merid, heat, tracer]

        @pl.when(jnp.logical_not(in_band))
        def _():
            for f in range(5):
                put(out_ref, (f, i), state[f] + time_step * rates[f])
            if first:
                zero = jnp.zeros((LEVELS, width), jnp.float32)
                put(scale_ref, (i,), zero)
                put(ones_ref, (i,), zero)

        @pl.when(in_band)
        def _():
            count = 6 if first else 5
            whole_scale = jnp.ones((LEVELS, LANES), jnp.float32)
            whole = [jnp.zeros((LEVELS, LANES), jnp.float32) for _ in range(count)]
            for k in range(chunks):
                low, high = k * LANES, (k + 1) * LANES
                last = k == chunks - 1
                decay = decay_tail_ref[r] if last else decay_ref[r, :, low:high]
                gain = jnp.sqrt(1.0 - decay * decay)
                offsets = [gain * x[:, low:high] for x in rates]
                if first:
                    offsets.append(gain)
                scale, offsets = lane_scan(decay, offsets, lane, 7)
                here = lane == k
                to_lane = (k + 1) % LANES
                whole_scale = jnp.where(here, pltpu.roll(scale, to_lane, axis=1), whole_scale)
                whole = [
                    jnp.where(here, pltpu.roll(o, to_lane, axis=1), w)
                    for o, w in zip(offsets, whole)
                ]
                end = cols if last else high
                n = end - low
                for f in range(5):
                    value = state[f][:, low:high] + amount * offsets[f]
                    out_ref[f, i, :, low:end] = value[:, :n]
                if first:
                    scale_ref[i, :, low:end] = scale[:, :n]
                    ones_ref[i, :, low:end] = (time_step - amount * offsets[5])[:, :n]
            whole_scale, whole = lane_scan(whole_scale, whole, lane, chunk_steps)
            start = lane == 0
            before = [jnp.where(start, 0.0, pltpu.roll(w, 1, axis=1)) for w in whole]
            for f in range(5):
                prefix_ref[f, i] = before[f]
            if first:
                prefix_scale_ref[i] = jnp.where(start, 1.0, pltpu.roll(whole_scale, 1, axis=1))
                prefix_ones_ref[i] = before[5]

        return carry

    lax.fori_loop(0, rows - 2 * EDGE if inner else 2 * EDGE, row, 0)


def apply_kernel(state_ref, scale_ref, ones_ref, edge_state_ref, edge_scale_ref, edge_ones_ref,
                 entry_ref, out_ref):
    rows = out_ref.shape[1]
    inner = (state_ref, scale_ref, ones_ref)
    edges = (edge_state_ref, edge_scale_ref, edge_ones_ref)
    lax.fori_loop(
        0, rows - 2 * EDGE, functools.partial(apply_row, *inner, entry_ref, out_ref, EDGE), 0
    )
    lax.fori_loop(0, EDGE, functools.partial(apply_row, *edges, entry_ref, out_ref, 0), 0)
    lax.fori_loop(
        EDGE,
        2 * EDGE,
        functools.partial(apply_row, *edges, entry_ref, out_ref, rows - 2 * EDGE),
        0,
    )


def apply_row(state_ref, scale_ref, ones_ref, entry_ref, out_ref, shift_by, i, carry):
    cols = state_ref.shape[3]
    main = cols // LANES * LANES
    chunks = main // LANES + 1

    r = i + shift_by
    for f in range(5):
        entry = entry_ref[f, r]
        panel = jnp.broadcast_to(entry[:, LANES - 1:], (LEVELS, LANES))
        for k in range(chunks):
            low = k * LANES
            end = min(low + LANES, cols)
            inflow = jnp.broadcast_to(entry[:, k:k + 1], (LEVELS, LANES))
            out_ref[f, r, :, low:end] = (
                state_ref[f, i, :, low:end]
                + scale_ref[i, :, low:end] * inflow[:, :end - low]
                + ones_ref[i, :, low:end] * panel[:, :end - low]
            )
    return carry


def caps_kernel(caps_ref, out_ref, send_sem, recv_sem):
    mine, count = lax.axis_index("lat"), lax.axis_size("lat")
    barrier = pltpu.get_barrier_semaphore()
    poles = (0, count - 1)

    def greet(pole):
        pl.semaphore_signal(
            barrier, inc=1, device_id={"lat": pole}, device_id_type=pl.DeviceIdType.MESH
        )

    def copy(side, other):
        return pltpu.make_async_remote_copy(
            src_ref=caps_ref.at[side],
            dst_ref=out_ref.at[side],
            send_sem=send_sem.at[other],
            recv_sem=recv_sem.at[side],
            device_id={"lat": other},
            device_id_type=pl.DeviceIdType.MESH,
        )

    for side, pole in enumerate(poles):
        pl.when(mine != pole)(functools.partial(greet, pole))
    for side, pole in enumerate(poles):

        @pl.when(mine == pole)
        def _():
            pl.semaphore_wait(barrier, count - 1)
            out_ref[side] = caps_ref[side]

            def start(step, carry):
                copy(side, lax.rem(pole + step, count)).start()
                return carry

            lax.fori_loop(1, count, start, 0)

    for side, pole in enumerate(poles):

        @pl.when(mine != pole)
        def _():
            copy(side, pole).wait_recv()

        @pl.when(mine == pole)
        def _():
            def finish(step, carry):
                copy(side, lax.rem(pole + step, count)).wait_send()
                return carry

            lax.fori_loop(1, count, finish, 0)


def share_caps(caps):
    return pl.pallas_call(
        caps_kernel,
        out_shape=shaped(caps.shape),
        in_specs=[pl.BlockSpec(memory_space=pltpu.VMEM)],
        out_specs=pl.BlockSpec(memory_space=pltpu.VMEM),
        scratch_shapes=[
            pltpu.SemaphoreType.DMA((lax.axis_size("lat"),)),
            pltpu.SemaphoreType.DMA((2,)),
        ],
        compiler_params=pltpu.CompilerParams(collective_id=0, has_side_effects=True),
    )(caps)


def level_block(shape):
    lead = len(shape) - 2
    return pl.BlockSpec(
        tuple(shape[:-2]) + (LEVELS, shape[-1]), lambda g: (0,) * lead + (g, 0)
    )


def shaped(shape):
    return jax.ShapeDtypeStruct(shape, jnp.float32)


def call_rates(first, band, table, state, tail, decay, decay_tail, halos=None):
    fields, rows, levels, cols = state.shape
    width = cols // LANES * LANES + LANES
    inner = halos is None
    count = rows - 2 * EDGE if inner else 2 * EDGE
    outs = [shaped((fields, count, levels, cols)), shaped((fields, count, levels, LANES))]
    if not inner:
        outs += [shaped((fields, 2, levels, LANES))]
    if first:
        outs += [shaped((count, levels, cols))] * 2 + [shaped((count, levels, LANES))] * 2
    arrays = (state, tail, decay, decay_tail) + (() if inner else halos)
    smem = pl.BlockSpec(memory_space=pltpu.SMEM)
    cells = fields * count * levels * cols
    return pl.pallas_call(
        functools.partial(rates_kernel, first, inner),
        grid=(levels // LEVELS,),
        in_specs=[smem, smem] + [level_block(x.shape) for x in arrays],
        out_specs=[level_block(x.shape) for x in outs],
        out_shape=outs,
        scratch_shapes=[pltpu.VMEM((4, rows + 4, LEVELS, width), jnp.float32)],
        compiler_params=pltpu.CompilerParams(vmem_limit_bytes=48 * 1024 * 1024),
        cost_estimate=pl.CostEstimate(
            flops=400 * cells, bytes_accessed=40 * cells, transcendentals=0
        ),
    )(band, table, *arrays)


def call_apply(inner, edges, entry):
    fields, rows, levels, _ = entry.shape
    cols = inner[0].shape[3]
    arrays = tuple(inner) + tuple(edges) + (entry,)
    out = shaped((fields, rows, levels, cols))
    return pl.pallas_call(
        apply_kernel,
        grid=(levels // LEVELS,),
        in_specs=[level_block(x.shape) for x in arrays],
        out_specs=level_block(out.shape),
        out_shape=out,
        compiler_params=pltpu.CompilerParams(vmem_limit_bytes=48 * 1024 * 1024),
    )(*arrays)


def join_rows(inner, edges, axis):
    first = lax.slice_in_dim(edges, 0, EDGE, axis=axis)
    last = lax.slice_in_dim(edges, EDGE, 2 * EDGE, axis=axis)
    return jnp.concatenate([first, inner, last], axis=axis)


def shift(x, axis, step, closed):
    count = lax.axis_size(axis)
    if closed:
        pairs = [(i, (i + step) % count) for i in range(count)]
    else:
        pairs = [(i, i + step) for i in range(count) if 0 <= i + step < count]
    return lax.ppermute(x, axis, pairs)


def lon_halos(state):
    cols = state.shape[3]
    head = jnp.moveaxis(state[..., :2], 3, 0)
    tail = jnp.moveaxis(state[..., cols - 2:], 3, 0)
    if lax.axis_size("lon") == 2:
        both = shift(jnp.concatenate([head, tail]), "lon", 1, True)
        west, east = both[2:], both[:2]
    else:
        west = shift(tail, "lon", 1, True)
        east = shift(head, "lon", -1, True)
    return jnp.moveaxis(west, 0, 3), jnp.moveaxis(east, 0, 3)


def lat_halos(state):
    rows = state.shape[1]

    def parts(strip):
        return jnp.stack(
            [strip[0], strip[0] * strip[2], strip[3] * strip[2], strip[4] * strip[2]]
        )

    south = shift(parts(state[:, rows - 2:]), "lat", 1, False)
    north = shift(parts(state[:, :2]), "lat", -1, False)
    return south, north


def over_lon(x):
    if lax.axis_size("lon") == 2:
        other = shift(x, "lon", 1, True)
        mine = lax.axis_index("lon") == 0
        return [jnp.where(mine, x, other), jnp.where(mine, other, x)]
    everything = lax.all_gather(x, "lon")
    return [everything[k] for k in range(lax.axis_size("lon"))]


def per_device(state, decay, band_rows):
    state = jnp.transpose(state, (0, 2, 1, 3))
    decay = jnp.transpose(decay, (1, 0, 2))
    fields, local_rows, levels, cols = state.shape
    lat_count, lon_count = lax.axis_size("lat"), lax.axis_size("lon")
    total_rows = local_rows * lat_count
    total_cols = cols * lon_count
    main = cols // LANES * LANES
    chunks = main // LANES + 1
    spare = main + LANES - cols - 4
    lat_index, lon_index = lax.axis_index("lat"), lax.axis_index("lon")
    rows = lat_index * local_rows + jnp.arange(local_rows, dtype=jnp.int32)
    centre = angles(2 * rows + 1, 2 * total_rows)
    cosine = jnp.sin(centre)
    sine = -jnp.cos(centre)
    face_rows = lat_index * local_rows + jnp.arange(local_rows + 1, dtype=jnp.int32)
    face_cos = jnp.sin(angles(face_rows, total_rows))
    low, high = face_cos[:-1], face_cos[1:]
    over = -1.0 / (12.0 * cosine)
    amount = time_step * cosine / edge_cosine
    table = jnp.stack(
        [
            low * over,
            (-high - 7.0 * low) * over,
            7.0 * (high - low) * over,
            (7.0 * high + low) * over,
            -high * over,
            over,
            coriolis * sine,
            amount,
        ],
        axis=1,
    )
    in_band = jnp.any(rows[:, None] == band_rows[None, :], axis=1)
    band = in_band.astype(jnp.int32)
    southern = rows < total_rows // 2
    decay_tail = jnp.pad(
        decay[:, :, main:], ((0, 0), (0, 0), (0, main + LANES - cols)), constant_values=1.0
    )
    lanes = jnp.arange(LANES)
    gap = jnp.zeros((fields, local_rows, levels, spare), jnp.float32)
    for substep in range(SUBSTEPS):
        south, north = lat_halos(state)
        west, east = lon_halos(state)
        tail = jnp.concatenate([state[..., main:], east, gap, west], axis=3)
        common = (substep == 0, band, table, state, tail, decay, decay_tail)
        inner = list(call_rates(*common))
        edges = list(call_rates(*common, halos=(south, north)))
        sums = edges.pop(2)
        prefix = join_rows(inner[1], edges[1], 1)
        if substep == 0:
            inner_maps, edge_maps = inner[2:4], edges[2:4]
            prefix_scale = join_rows(inner[4], edges[4], 0)
            prefix_ones = join_rows(inner[5], edges[5], 0)
        caps = share_caps(jnp.moveaxis(jnp.sum(sums, axis=-1), 1, 0))
        maps = jnp.concatenate(
            [
                prefix[..., chunks],
                prefix_scale[None, ..., chunks],
                prefix_ones[None, ..., chunks],
                jnp.where(southern[None, :, None], caps[0][:, None], caps[1][:, None]),
            ]
        )
        maps = over_lon(maps)
        panel = sum(x[7:] for x in maps) / total_cols
        pre_scale, pre_offset = jnp.ones_like(maps[0][:1]), jnp.zeros_like(panel)
        all_scale, all_offset = pre_scale, pre_offset
        for k in range(lon_count):
            step_scale = maps[k][5:6]
            step_offset = maps[k][:5] - panel * maps[k][6:7]
            all_offset = step_scale * all_offset + step_offset
            all_scale = step_scale * all_scale
            reached = k < lon_index
            pre_scale = jnp.where(reached, all_scale, pre_scale)
            pre_offset = jnp.where(reached, all_offset, pre_offset)
        inflow = pre_scale * (all_offset / (1.0 - all_scale)) + pre_offset
        entry = amount[:, None, None] * (
            prefix
            + prefix_scale[None] * inflow[..., None]
            - panel[..., None] * prefix_ones[None]
        )
        entry = jnp.where(lanes == LANES - 1, panel[..., None], entry)
        entry = jnp.where(in_band[:, None, None], entry, 0.0)
        state = call_apply([inner[0]] + inner_maps, [edges[0]] + edge_maps, entry)
    return jnp.transpose(state, (0, 2, 1, 3))


def solution(mesh):
    placed = (P(None, None, "lat", "lon"), P(None, "lat", "lon"), P())
    return jax.shard_map(
        per_device,
        mesh=mesh,
        in_specs=placed,
        out_specs=P(None, None, "lat", "lon"),
        check_vma=False,
    )
```
